32 devices in a mesh: groups: 2 (over x), mom: 4 (over y, core), en: 4 (over z).
Axes of the slice: x: 2, y: 2, z: 4, core: 2. Of those that a mesh axis runs over, the one named last changes fastest.
Arguments:
- green_blocks: bfloat16 [16, 8, 2, 2, 256, 256], P(('groups', 'mom'), 'en'), parts along dimension 0, may hold values from -6 to 6
- hopping: bfloat16 [6, 256, 256], P('groups'), parts along dimension 0, may hold values from -0.375 to 0.375
- phonons: bfloat16 [16, 3, 2, 256, 256], P(('groups', 'en')), parts along dimension 0, may hold values from -1.796875 to 1.796875
- phonon_pick: int32 [4], replicated, may hold values from 0 to 7
- momentum_offsets: int32 [4, 8], P(None, 'mom'), may hold values from 0 to 1
- energy_map: int32 [4, 8], P(None, 'en'), may hold values from 0 to 1
Outputs:
- self_energy: float32 [16, 8, 2, 2, 256, 256], P(('groups', 'mom'), 'en'), parts along dimension 0
The draws below stay inside these ranges and needn't reach their ends.
There are 2 independent parts, one for each index of `groups`. The reference program is written for one: setup_inputs(seed, part) draws one part's arguments, and reference() takes and returns one part's arrays. A program takes and returns all parts, laid end to end along the dimension named above; an argument that names none is the same for every part. Nothing has to cross between parts.
All inputs are finite; a program needn't handle non-finite values.
Results may differ from the reference program's by a relative error of at most 0.0029.
Values may be sent and summed in bfloat16 or wider, within the bound.
A program may use at most 128 MiB of HBM per device.

```python
import jax
import jax.numpy as jnp
from jax import lax

NO = 256
CELLS = 2
MODES = 3
K_DEV = 2
E_DEV = 2
STEPS = 4
MOMENTA = 8
ENERGIES = 8
POINTS = 8


def with_ends(array, rng, low, top_value):
    dims = array.shape
    index_at = [jax.random.randint(jax.random.fold_in(rng, axis), (), 0, dims[axis]) for axis in range(len(dims))]
    array = array.at[tuple(index_at)].set(low)
    longest = dims.index(max(dims))
    index_at[longest] = (index_at[longest] + 1) % dims[longest]
    return array.at[tuple(index_at)].set(top_value)


def shard_levels(key, dims, split, smallest, high):
    def one(position, blocks):
        steps = jax.random.uniform(jax.random.fold_in(jax.random.fold_in(key, 6), position), (blocks,), jnp.float32, smallest / len(split), high / len(split))
        return jnp.repeat(jnp.exp(steps), dims[position] // blocks).reshape((-1,) + (1,) * (len(dims) - position - 1))

    loudness = one(*split[0])
    for cut in split[1:]:
        loudness = loudness * one(*cut)
    return loudness


def bell_draw(key, dims, spread, most, cuts=(), kind=jnp.bfloat16):
    factor_of = shard_levels(key, dims, cuts, -0.22, 0.18) if cuts else 1.0
    result = jax.random.normal(key, dims, jnp.float32) * spread * factor_of
    return jnp.minimum(jnp.maximum(result, -most), most).astype(kind)


def setup_inputs(seed: int = 0, part: int = 0) -> dict:
    key_list = jax.random.split(jax.random.key(seed), 7)
    own_keys = jax.random.split(jax.random.fold_in(key_list[6], part), 7)
    green_blocks = bell_draw(own_keys[0], (MOMENTA, ENERGIES, CELLS, 2, NO, NO), 1.0, 6.0, ((0, 4), (1, 4)))
    hopping = bell_draw(own_keys[1], (MODES, NO, NO), NO ** -0.5, 0.375)
    phonons = bell_draw(own_keys[2], (POINTS, MODES, 2, NO, NO), 0.3, 1.796875, ((0, 4),))
    phonon_pick = with_ends(jax.random.randint(key_list[3], (STEPS,), 0, POINTS), jax.random.fold_in(key_list[3], 1), 0, POINTS - 1).astype(jnp.int32)
    momentum_offsets = with_ends(jax.random.randint(key_list[4], (STEPS, MOMENTA), 0, K_DEV), jax.random.fold_in(key_list[4], 1), 0, K_DEV - 1).astype(jnp.int32)
    energy_map = with_ends(jax.random.randint(key_list[5], (STEPS, ENERGIES), 0, E_DEV), jax.random.fold_in(key_list[5], 1), 0, E_DEV - 1).astype(jnp.int32)
    return {"green_blocks": green_blocks, "hopping": hopping, "phonons": phonons, "phonon_pick": phonon_pick, "momentum_offsets": momentum_offsets, "energy_map": energy_map}


momentum_hops = (1, -1, 2, -2)


def reference(green_blocks, hopping, phonons, phonon_pick, momentum_offsets, energy_map):
    hopping_wide = hopping.astype(jnp.float32)
    energy_index = jnp.arange(ENERGIES, dtype=jnp.int32)
    energy_rows = (energy_index - energy_index % E_DEV)[None, :] + energy_map

    def per_momentum(momentum):
        accumulated = jnp.zeros((ENERGIES, CELLS, 2, NO, NO), jnp.float32)
        for step_index in range(STEPS):
            hop_value = momentum_hops[step_index]
            source_row = ((momentum - momentum % K_DEV - hop_value * K_DEV) % MOMENTA + momentum_offsets[step_index, momentum]).astype(jnp.int32)
            green_rows = lax.dynamic_index_in_dim(green_blocks, source_row, 0, keepdims=False)
            chosen = jnp.take(green_rows, energy_rows[step_index], axis=0).astype(jnp.float32)
            left_product = jnp.einsum('aij,ecpjk->aecpik', hopping_wide, chosen)
            left_product = lax.optimization_barrier(left_product.astype(jnp.bfloat16)).astype(jnp.float32)
            right_product = jnp.einsum('aecpij,ajk->aecpik', left_product, hopping_wide)
            coupling = phonons[phonon_pick[step_index]].astype(jnp.float32)
            coupling_real = coupling[:, 0][:, None, None]
            coupling_imag = coupling[:, 1][:, None, None]
            right_real = right_product[:, :, :, 0]
            right_imag = right_product[:, :, :, 1]
            real_part = jnp.sum(right_real * coupling_real - right_imag * coupling_imag, axis=0)
            imag_part = jnp.sum(right_real * coupling_imag + right_imag * coupling_real, axis=0)
            accumulated = accumulated + jnp.stack([real_part, imag_part], axis=2)
        return accumulated

    return lax.map(per_momentum, jnp.arange(MOMENTA, dtype=jnp.int32))
```

```python
import functools

import jax
import jax.numpy as jnp
from jax import lax
from jax.experimental import pallas as pl
from jax.experimental.pallas import tpu as pltpu
from jax.sharding import PartitionSpec as P

STEPS = 4
LAG = 2
MESH = pl.DeviceIdType.MESH


def kernel(
    n_mom, n_en, pick_ref, mom_ref, map_ref, green, hop, phon, out,
    near, low, top, right_in, left_in, weights,
    far_s, far_r, high_s, high_r, own_s, own_r, pass_s, pass_r,
    rt_s, rt_r, lt_s, lt_r, half_s, half_r,
):
    mom, z = lax.axis_index("mom"), lax.axis_index("en")
    core = lax.rem(mom, 2)
    sibling = mom + 1 - 2 * core
    up = lax.rem(mom + 2, n_mom)
    down = lax.rem(mom + n_mom - 2, n_mom)
    two = n_mom == 4
    slots, modes, _, rows, cols = phon.shape
    pieces = len(near)
    half = rows // 2
    mine = pl.ds(pl.multiple_of(core * half, half), half)
    chunks = STEPS * modes
    last = n_en - 1

    barrier = pltpu.get_barrier_semaphore()
    for other in (sibling, up) if two else (sibling, up, down):
        pl.semaphore_signal(barrier, inc=1, device_id={"mom": other}, device_id_type=MESH)

    @pl.when(z > 0)
    def _():
        pl.semaphore_signal(barrier, inc=1, device_id={"en": z - 1}, device_id_type=MESH)

    @pl.when(z < last)
    def _():
        pl.semaphore_signal(barrier, inc=1, device_id={"en": z + 1}, device_id_type=MESH)

    out[...] = jnp.zeros_like(out)
    greeted = (2 if two else 3) + (z > 0).astype(jnp.int32) + (z < last).astype(jnp.int32)
    pl.semaphore_wait(barrier, greeted)

    def remote(src, dst, send, recv, **device):
        return pltpu.make_async_remote_copy(
            src_ref=src, dst_ref=dst, send_sem=send, recv_sem=recv, device_id=device, device_id_type=MESH
        )

    def part(i):
        return green.at[:, :, i // 2, i % 2]

    def far(i):
        return remote(part(i), low[i], far_s.at[i], far_r.at[i], mom=up)

    def high(i):
        return remote(part(i), top[i], high_s.at[i], high_r.at[i], mom=down)

    def own(i):
        return remote(part(i), near[i].at[core], own_s.at[i], own_r.at[i], mom=sibling)

    def passed(i, source):
        return remote((low if source == 2 else top)[i], near[i].at[1 - core], pass_s.at[i], pass_r.at[i], mom=sibling)

    def rightward(q):
        return remote(right_in.at[q], right_in.at[q], rt_s.at[q], rt_r.at[q], en=z + 1)

    def leftward(q):
        return remote(left_in.at[q], left_in.at[q], lt_s.at[q], lt_r.at[q], en=z - 1)

    def share(q):
        return remote(weights.at[q, :, mine], weights.at[q, :, mine], half_s.at[q], half_r.at[q], mom=sibling)

    for i in range(pieces):
        far(i).start()
        if not two:
            high(i).start()
    for i in range(pieces):
        own(i).start()

    def forward(i):
        far(i).wait_recv()
        if two:
            passed(i, 2).start()
        else:
            high(i).wait_recv()

            @pl.when(core == 0)
            def _():
                passed(i, 3).start()

            @pl.when(core == 1)
            def _():
                passed(i, 2).start()

    def mix(q, buffer, at_end, arrival):
        point = pick_ref[q // modes]
        local = phon[lax.rem(point, slots), lax.rem(q, modes), :, mine]

        @pl.when(at_end)
        def _():
            buffer[q] = local

        @pl.when(jnp.logical_not(at_end))
        def _():
            arrival(q).wait_recv()
            buffer[q] = jnp.where(lax.div(point, slots) == z, local, buffer[q])

    def tick(t):
        q_right = t - LAG * z
        q_left = t - LAG * (last - z)
        q_done = t - LAG * jnp.maximum(z, last - z)

        @pl.when((q_right >= 0) & (q_right < chunks))
        def _():
            mix(q_right, right_in, z == 0, rightward)

            @pl.when(z < last)
            def _():
                rightward(q_right).start()

        @pl.when((q_left >= 0) & (q_left < chunks))
        def _():
            mix(q_left, left_in, z == last, leftward)

            @pl.when(z > 0)
            def _():
                leftward(q_left).start()

        @pl.when((q_done >= 0) & (q_done < chunks))
        def _():
            owner = lax.div(pick_ref[q_done // modes], slots)
            weights[q_done, :, mine] = jnp.where(owner <= z, right_in[q_done], left_in[q_done])
            share(q_done).start()

    def unit(step, i):
        source = 2 if two and step == 3 else step
        cell, imag = i // 2, i % 2

        def pair(j, carry):
            k, e = j // 2, j % 2
            m, n = mom_ref[step, k], map_ref[step, e]
            block = near[i][step, m, n] if step < 2 else (low if source == 2 else top)[i][m, n]
            real_sum = out[k, e, cell, 0]
            imag_sum = out[k, e, cell, 1]
            for a in range(modes):
                left = jnp.dot(hop[a], block, preferred_element_type=jnp.float32).astype(jnp.bfloat16)
                right = jnp.dot(left, hop[a], preferred_element_type=jnp.float32)
                w_re = weights[step * modes + a, 0].astype(jnp.float32)
                w_im = weights[step * modes + a, 1].astype(jnp.float32)
                if imag:
                    real_sum = real_sum - right * w_im
                    imag_sum = imag_sum + right * w_re
                else:
                    real_sum = real_sum + right * w_re
                    imag_sum = imag_sum + right * w_im
            out[k, e, cell, 0] = real_sum
            out[k, e, cell, 1] = imag_sum
            return carry

        lax.fori_loop(0, 4, pair, 0)

    seen = set()

    def need(step, i):
        if ("w", step) not in seen:
            seen.add(("w", step))
            for a in range(modes):
                share(step * modes + a).wait_recv()
        if step < 2 and ("g", i) not in seen:
            seen.add(("g", i))
            own(i).wait_recv()
            passed(i, 2).wait_recv()

    base = LAG * last + modes
    forwards = {base - 4: 0, base: 1, base + 4: 2, base + 8: 3}
    order = [
        (0, 0), (0, 1), (1, 0), (1, 1), None, (2, 0), (2, 1), (0, 2), (1, 2), (2, 2),
        (3, 0), (3, 1), (3, 2), (2, 3), (3, 3), (0, 3), (1, 3),
    ]
    sent = 0
    total = chunks + LAG * last
    for t in range(max(total, base + len(order))):
        if t < total:
            tick(t)
        if t in forwards:
            forward(forwards[t])
        if 0 <= t - base < len(order) and order[t - base]:
            step, i = order[t - base]
            need(step, i)
            unit(step, i)

    for i in range(pieces):
        far(i).wait_send()
        own(i).wait_send()
        passed(i, 2).wait_send()
        if not two:
            high(i).wait_send()

    def settle(q, carry):
        @pl.when(z < last)
        def _():
            rightward(q).wait_send()

        @pl.when(z > 0)
        def _():
            leftward(q).wait_send()

        share(q).wait_send()
        return carry

    lax.fori_loop(0, chunks, settle, 0)


def on_device(green_blocks, hopping, phonons, phonon_pick, momentum_offsets, energy_map):
    modes = hopping.shape[0]
    rows, cols = hopping.shape[1:]
    k_dev, e_dev, cells, parts = green_blocks.shape[:4]
    pieces = cells * parts
    chunks = STEPS * modes
    two = lax.axis_size("mom") == 4
    dma = pltpu.SemaphoreType.DMA
    vmem = pl.BlockSpec(memory_space=pltpu.VMEM)
    smem = pl.BlockSpec(memory_space=pltpu.SMEM)
    return pl.pallas_call(
        functools.partial(kernel, lax.axis_size("mom"), lax.axis_size("en")),
        out_shape=jax.ShapeDtypeStruct(green_blocks.shape, jnp.float32),
        in_specs=[smem, smem, smem, pl.BlockSpec(memory_space=pl.ANY), vmem, vmem],
        out_specs=vmem,
        scratch_shapes=[
            [pltpu.VMEM((2, k_dev, e_dev, rows, cols), jnp.bfloat16)] * pieces,
            [pltpu.VMEM((k_dev, e_dev, rows, cols), jnp.bfloat16)] * pieces,
            [pltpu.VMEM((k_dev, e_dev, rows, cols), jnp.bfloat16)] * (0 if two else pieces),
            pltpu.VMEM((chunks, 2, rows // 2, cols), jnp.bfloat16),
            pltpu.VMEM((chunks, 2, rows // 2, cols), jnp.bfloat16),
            pltpu.VMEM((chunks, 2, rows, cols), jnp.bfloat16),
        ]
        + [dma((pieces,))] * 8
        + [dma((chunks,))] * 6,
        compiler_params=pltpu.CompilerParams(
            collective_id=0, has_side_effects=True, vmem_limit_bytes=48 * 2**20
        ),
        cost_estimate=pl.CostEstimate(flops=13 * 10**9, bytes_accessed=8 * 2**20, transcendentals=0),
    )(phonon_pick, momentum_offsets, energy_map, green_blocks, hopping, phonons)


def solution(mesh):
    placed = (
        P(("groups", "mom"), "en", None, None, None, None),
        P("groups", None, None),
        P(("groups", "en"), None, None, None, None),
        P(),
        P(None, "mom"),
        P(None, "en"),
    )
    return jax.shard_map(
        on_device,
        mesh=mesh,
        in_specs=placed,
        out_specs=P(("groups", "mom"), "en", None, None, None, None),
        check_vma=False,
    )
```

```python
import functools

import jax
import jax.numpy as jnp
from jax import lax
from jax.experimental import pallas as pl
from jax.experimental.pallas import tpu as pltpu
from jax.sharding import PartitionSpec as P

STEPS = 4
LAG = 2
STRIP = 16
MESH = pl.DeviceIdType.MESH


def kernel(
    n_mom, n_en, pick_in, mom_in, map_in, green, hop_in, phon_in, out,
    pick_ref, mom_ref, map_ref, hop, phon, near, low, top, low_t, top_t, own_t, near_t,
    right_in, left_in, weights, load,
    far_s, far_r, high_s, high_r, own_s, own_r, pass_s, pass_r,
    rt_s, rt_r, lt_s, lt_r, half_s, half_r,
):
    mom, z = lax.axis_index("mom"), lax.axis_index("en")
    core = lax.rem(mom, 2)
    sibling = mom + 1 - 2 * core
    up = lax.rem(mom + 2, n_mom)
    down = lax.rem(mom + n_mom - 2, n_mom)
    two = n_mom == 4
    slots, modes, _, rows, cols = phon_in.shape
    pieces = len(near)
    half = rows // 2
    mine = pl.ds(pl.multiple_of(core * half, half), half)
    chunks = STEPS * modes
    last = n_en - 1

    loads = [
        pltpu.make_async_copy(src, dst, load.at[i])
        for i, (src, dst) in enumerate(
            ((pick_in, pick_ref), (phon_in.at[:, :, :, mine], phon), (mom_in, mom_ref), (map_in, map_ref), (hop_in, hop))
        )
    ]
    for copy in loads:
        copy.start()

    barrier = pltpu.get_barrier_semaphore()
    for other in (sibling, up) if two else (sibling, up, down):
        pl.semaphore_signal(barrier, inc=1, device_id={"mom": other}, device_id_type=MESH)

    @pl.when(z > 0)
    def _():
        pl.semaphore_signal(barrier, inc=1, device_id={"en": z - 1}, device_id_type=MESH)

    @pl.when(z < last)
    def _():
        pl.semaphore_signal(barrier, inc=1, device_id={"en": z + 1}, device_id_type=MESH)

    out[...] = jnp.zeros_like(out)
    greeted = (2 if two else 3) + (z > 0).astype(jnp.int32) + (z < last).astype(jnp.int32)
    pl.semaphore_wait(barrier, greeted)

    def remote(src, dst, send, recv, **device):
        return pltpu.make_async_remote_copy(
            src_ref=src, dst_ref=dst, send_sem=send, recv_sem=recv, device_id=device, device_id_type=MESH
        )

    def part(i):
        return green.at[:, :, i // 2, i % 2]

    def far(i):
        return remote(part(i), low[i], far_s.at[i], far_r.at[i], mom=up)

    def high(i):
        return remote(part(i), top[i], high_s.at[i], high_r.at[i], mom=down)

    def own(i):
        return remote(part(i), near[i].at[0], own_s.at[i], own_r.at[i], mom=sibling)

    def passed(i, source):
        return remote((low if source == 2 else top)[i], near[i].at[1], pass_s.at[i], pass_r.at[i], mom=sibling)

    def rightward(q):
        return remote(right_in.at[q], right_in.at[q], rt_s.at[q], rt_r.at[q], en=z + 1)

    def leftward(q):
        return remote(left_in.at[q], left_in.at[q], lt_s.at[q], lt_r.at[q], en=z - 1)

    def share(q):
        return remote(weights.at[q, :, mine], weights.at[q, :, mine], half_s.at[q], half_r.at[q], mom=sibling)

    for i in range(pieces):
        far(i).start()
        if not two:
            high(i).start()
    for i in range(pieces):
        own(i).start()
    loads[0].wait()
    loads[1].wait()

    def forward(i):
        far(i).wait_recv()
        if two:
            passed(i, 2).start()
        else:
            high(i).wait_recv()

            @pl.when(core == 0)
            def _():
                passed(i, 3).start()

            @pl.when(core == 1)
            def _():
                passed(i, 2).start()

    def mix(q, buffer, at_end, arrival):
        point = pick_ref[q // modes]
        local = phon[lax.rem(point, slots), lax.rem(q, modes)]

        @pl.when(at_end)
        def _():
            buffer[q] = local

        @pl.when(jnp.logical_not(at_end))
        def _():
            arrival(q).wait_recv()
            buffer[q] = jnp.where(lax.div(point, slots) == z, local, buffer[q])

    def tick(t):
        q_right = t - LAG * z
        q_left = t - LAG * (last - z)
        q_done = t - LAG * jnp.maximum(z, last - z)

        @pl.when((q_right >= 0) & (q_right < chunks))
        def _():
            mix(q_right, right_in, z == 0, rightward)

            @pl.when(z < last)
            def _():
                rightward(q_right).start()

        @pl.when((q_left >= 0) & (q_left < chunks))
        def _():
            mix(q_left, left_in, z == last, leftward)

            @pl.when(z > 0)
            def _():
                leftward(q_left).start()

        @pl.when((q_done >= 0) & (q_done < chunks))
        def _():
            owner = lax.div(pick_ref[q_done // modes], slots)
            weights[q_done, :, mine] = jnp.where(owner <= z, right_in[q_done], left_in[q_done])
            share(q_done).start()

    def transform(source, turned):
        def block(m, carry):
            left = [
                jnp.dot(hop[...], source[m, n], preferred_element_type=jnp.float32).astype(jnp.bfloat16)
                for n in range(2)
            ]
            for a in range(modes):
                span = slice(a * rows, (a + 1) * rows)
                for n in range(2):
                    turned[a, m, n] = jnp.dot(left[n][span], hop[span], preferred_element_type=jnp.float32)
            return carry

        lax.fori_loop(0, 2, block, 0)

    def weigh(turned, step, i):
        cell, imag = i // 2, i % 2

        def strip(r, carry):
            span = pl.ds(pl.multiple_of(r * STRIP, STRIP), STRIP)
            w = [[weights[step * modes + a, p, span].astype(jnp.float32) for p in range(2)] for a in range(modes)]
            for k in range(2):
                for e in range(2):
                    m, n = mom_ref[k, step], map_ref[e, step]
                    t = [turned[a, m, n, span] for a in range(modes)]
                    with_re = sum(t[a] * w[a][0] for a in range(modes))
                    with_im = sum(t[a] * w[a][1] for a in range(modes))
                    if imag:
                        out[k, e, cell, 0, span] -= with_im
                        out[k, e, cell, 1, span] += with_re
                    else:
                        out[k, e, cell, 0, span] += with_re
                        out[k, e, cell, 1, span] += with_im
            return carry

        lax.fori_loop(0, rows // STRIP, strip, 0)

    def far_turn(i):
        transform(low[i], low_t[i])
        if not two:
            transform(top[i], top_t[i])

    def third(i):
        weigh(low_t[i], 2, i)

    def fourth(i):
        weigh(low_t[i] if two else top_t[i], 3, i)

    def own_turn(i):
        own(i).wait_recv()
        transform(near[i].at[0], own_t[i] if two else near_t)

    def own_weigh(i):
        if not two:
            own_turn(i)
        weigh(own_t[i] if two else near_t, 1 - core, i)

    def sibling_far(i):
        passed(i, 2).wait_recv()
        transform(near[i].at[1], near_t)
        weigh(near_t, core, i)

    def arrived(step):
        for a in range(modes):
            share(step * modes + a).wait_recv()

    base = LAG * last + modes
    total = chunks + LAG * last
    plan = {
        base - 3: [(forward, 0)],
        base - 2: [(far_turn, 0)],
        base: [(arrived, 0)],
        base + 2: [(forward, 1), (far_turn, 1)],
        base + 3: [(arrived, 1), (own_weigh, 0), (own_weigh, 1), (sibling_far, 0)],
        base + 4: [(own_weigh, 2), (own_weigh, 3)],
        base + 5: [(sibling_far, 1)],
        base + 6: [(arrived, 2), (forward, 2), (third, 0)],
        base + 7: [(far_turn, 2), (third, 1)],
        base + 8: [(third, 2)],
        base + 9: [
            (sibling_far, 2), (arrived, 3), (fourth, 0), (fourth, 1), (fourth, 2),
            (forward, 3), (far_turn, 3), (third, 3), (fourth, 3), (sibling_far, 3),
        ],
    }
    if two:
        plan.update({1 + i: [(own_turn, i)] for i in range(pieces)})
    for copy in loads[2:]:
        copy.wait()
    for t in range(max(total, base + 10)):
        if t < total:
            tick(t)
        for task, which in plan.get(t, []):
            task(which)

    for i in range(pieces):
        far(i).wait_send()
        own(i).wait_send()
        passed(i, 2).wait_send()
        if not two:
            high(i).wait_send()

    def settle(q, carry):
        @pl.when(z < last)
        def _():
            rightward(q).wait_send()

        @pl.when(z > 0)
        def _():
            leftward(q).wait_send()

        share(q).wait_send()
        return carry

    lax.fori_loop(0, chunks, settle, 0)


def on_device(green_blocks, hopping, phonons, phonon_pick, momentum_offsets, energy_map):
    modes = hopping.shape[0]
    rows, cols = hopping.shape[1:]
    k_dev, e_dev, cells, parts = green_blocks.shape[:4]
    pieces = cells * parts
    chunks = STEPS * modes
    two = lax.axis_size("mom") == 4
    dma = pltpu.SemaphoreType.DMA
    vmem = pl.BlockSpec(memory_space=pltpu.VMEM)
    hbm = pl.BlockSpec(memory_space=pl.ANY)
    turned = pltpu.VMEM((modes, k_dev, e_dev, rows, cols), jnp.float32)
    return pl.pallas_call(
        functools.partial(kernel, lax.axis_size("mom"), lax.axis_size("en")),
        out_shape=jax.ShapeDtypeStruct(green_blocks.shape, jnp.float32),
        in_specs=[hbm] * 6,
        out_specs=vmem,
        scratch_shapes=[
            pltpu.SMEM(phonon_pick.shape, jnp.int32),
            pltpu.SMEM(momentum_offsets.shape[::-1], jnp.int32),
            pltpu.SMEM(energy_map.shape[::-1], jnp.int32),
            pltpu.VMEM((modes * rows, cols), jnp.bfloat16),
            pltpu.VMEM((*phonons.shape[:3], rows // 2, cols), jnp.bfloat16),
            [pltpu.VMEM((2, k_dev, e_dev, rows, cols), jnp.bfloat16)] * pieces,
            [pltpu.VMEM((k_dev, e_dev, rows, cols), jnp.bfloat16)] * pieces,
            [pltpu.VMEM((k_dev, e_dev, rows, cols), jnp.bfloat16)] * (0 if two else pieces),
            [turned] * pieces,
            [turned] * (0 if two else pieces),
            [turned] * (pieces if two else 0),
            turned,
            pltpu.VMEM((chunks, 2, rows // 2, cols), jnp.bfloat16),
            pltpu.VMEM((chunks, 2, rows // 2, cols), jnp.bfloat16),
            pltpu.VMEM((chunks, 2, rows, cols), jnp.bfloat16),
            dma((5,)),
        ]
        + [dma((pieces,))] * 8
        + [dma((chunks,))] * 6,
        compiler_params=pltpu.CompilerParams(
            collective_id=0, has_side_effects=True, vmem_limit_bytes=(59 if two else 60) * 2**20
        ),
        cost_estimate=pl.CostEstimate(flops=13 * 10**9, bytes_accessed=8 * 2**20, transcendentals=0),
    )(
        phonon_pick, momentum_offsets.T, energy_map.T, green_blocks, hopping.reshape(-1, cols), phonons
    )


def solution(mesh):
    placed = (
        P(("groups", "mom"), "en", None, None, None, None),
        P("groups", None, None),
        P(("groups", "en"), None, None, None, None),
        P(),
        P(None, "mom"),
        P(None, "en"),
    )
    return jax.shard_map(
        on_device,
        mesh=mesh,
        in_specs=placed,
        out_specs=P(("groups", "mom"), "en", None, None, None, None),
        check_vma=False,
    )
```

```python
import functools

import jax
import jax.numpy as jnp
from jax import lax
from jax.experimental import pallas as pl
from jax.experimental.pallas import tpu as pltpu
from jax.sharding import PartitionSpec as P

STEPS = 4
LAG = 2
STRIP = 16
MESH = pl.DeviceIdType.MESH


def kernel(
    n_mom, n_en, pick_in, mom_in, map_in, green, hop_in, phon_in, out,
    pick_ref, mom_ref, map_ref, hop, phon, near, low, top, low_t, top_t, own_t, near_t,
    right_in, left_in, weights, load,
    far_s, far_r, high_s, high_r, own_s, own_r, pass_s, pass_r,
    rt_s, rt_r, lt_s, lt_r, half_s, half_r,
):
    mom, z = lax.axis_index("mom"), lax.axis_index("en")
    core = lax.rem(mom, 2)
    sibling = mom + 1 - 2 * core
    up = lax.rem(mom + 2, n_mom)
    down = lax.rem(mom + n_mom - 2, n_mom)
    two = n_mom == 4
    slots, modes, _, rows, cols = phon_in.shape
    pieces = len(near)
    half = rows // 2
    mine = pl.ds(pl.multiple_of(core * half, half), half)
    chunks = STEPS * modes
    last = n_en - 1

    loads = [
        pltpu.make_async_copy(src, dst, load.at[i])
        for i, (src, dst) in enumerate(
            ((pick_in, pick_ref), (phon_in.at[:, :, :, mine], phon), (mom_in, mom_ref), (map_in, map_ref), (hop_in, hop))
        )
    ]
    for copy in loads:
        copy.start()

    barrier = pltpu.get_barrier_semaphore()
    for other in (sibling, up) if two else (sibling, up, down):
        pl.semaphore_signal(barrier, inc=1, device_id={"mom": other}, device_id_type=MESH)

    @pl.when(z > 0)
    def _():
        pl.semaphore_signal(barrier, inc=1, device_id={"en": z - 1}, device_id_type=MESH)

    @pl.when(z < last)
    def _():
        pl.semaphore_signal(barrier, inc=1, device_id={"en": z + 1}, device_id_type=MESH)

    out[...] = jnp.zeros_like(out)
    greeted = (2 if two else 3) + (z > 0).astype(jnp.int32) + (z < last).astype(jnp.int32)
    pl.semaphore_wait(barrier, greeted)

    def remote(src, dst, send, recv, **device):
        return pltpu.make_async_remote_copy(
            src_ref=src, dst_ref=dst, send_sem=send, recv_sem=recv, device_id=device, device_id_type=MESH
        )

    def part(i):
        return green.at[:, :, i // 2, i % 2]

    def far(i):
        return remote(part(i), low[i], far_s.at[i], far_r.at[i], mom=up)

    def high(i):
        return remote(part(i), top[i], high_s.at[i], high_r.at[i], mom=down)

    def own(i):
        return remote(part(i), near[i].at[0], own_s.at[i], own_r.at[i], mom=sibling)

    def passed(i, source):
        return remote((low if source == 2 else top)[i], near[i].at[1], pass_s.at[i], pass_r.at[i], mom=sibling)

    def rightward(q):
        return remote(right_in.at[q], right_in.at[q], rt_s.at[q], rt_r.at[q], en=z + 1)

    def leftward(q):
        return remote(left_in.at[q], left_in.at[q], lt_s.at[q], lt_r.at[q], en=z - 1)

    def share(q):
        return remote(weights.at[q, :, mine], weights.at[q, :, mine], half_s.at[q], half_r.at[q], mom=sibling)

    for i in range(pieces):
        far(i).start()
        if not two:
            high(i).start()
    for i in range(pieces):
        own(i).start()
    loads[0].wait()
    loads[1].wait()

    def forward(i):
        far(i).wait_recv()
        if two:
            passed(i, 2).start()
        else:
            high(i).wait_recv()

            @pl.when(core == 0)
            def _():
                passed(i, 3).start()

            @pl.when(core == 1)
            def _():
                passed(i, 2).start()

    def mix(q, buffer, at_end, arrival):
        point = pick_ref[q // modes]
        local = phon[lax.rem(point, slots), lax.rem(q, modes)]

        @pl.when(at_end)
        def _():
            buffer[q] = local

        @pl.when(jnp.logical_not(at_end))
        def _():
            arrival(q).wait_recv()
            buffer[q] = jnp.where(lax.div(point, slots) == z, local, buffer[q])

    def tick(t):
        q_right = t - LAG * z
        q_left = t - LAG * (last - z)
        q_done = t - LAG * jnp.maximum(z, last - z)

        @pl.when((q_right >= 0) & (q_right < chunks))
        def _():
            mix(q_right, right_in, z == 0, rightward)

            @pl.when(z < last)
            def _():
                rightward(q_right).start()

        @pl.when((q_left >= 0) & (q_left < chunks))
        def _():
            mix(q_left, left_in, z == last, leftward)

            @pl.when(z > 0)
            def _():
                leftward(q_left).start()

        @pl.when((q_done >= 0) & (q_done < chunks))
        def _():
            owner = lax.div(pick_ref[q_done // modes], slots)
            weights[q_done, :, mine] = jnp.where(owner <= z, right_in[q_done], left_in[q_done])
            share(q_done).start()

    def transform(source, turned):
        def block(m, carry):
            left = [
                jnp.dot(hop[...], source[m, n], preferred_element_type=jnp.float32).astype(jnp.bfloat16)
                for n in range(2)
            ]
            for a in range(modes):
                span = slice(a * rows, (a + 1) * rows)
                for n in range(2):
                    turned[a, m, n] = jnp.dot(left[n][span], hop[span], preferred_element_type=jnp.float32)
            return carry

        lax.fori_loop(0, 2, block, 0)

    def weigh(turned, step, i):
        cell, imag = i // 2, i % 2

        def strip(r, carry):
            span = pl.ds(pl.multiple_of(r * STRIP, STRIP), STRIP)
            w = [[weights[step * modes + a, p, span].astype(jnp.float32) for p in range(2)] for a in range(modes)]
            for k in range(2):
                for e in range(2):
                    m, n = mom_ref[k, step], map_ref[e, step]
                    t = [turned[a, m, n, span] for a in range(modes)]
                    with_re = sum(t[a] * w[a][0] for a in range(modes))
                    with_im = sum(t[a] * w[a][1] for a in range(modes))
                    if imag:
                        out[k, e, cell, 0, span] -= with_im
                        out[k, e, cell, 1, span] += with_re
                    else:
                        out[k, e, cell, 0, span] += with_re
                        out[k, e, cell, 1, span] += with_im
            return carry

        lax.fori_loop(0, rows // STRIP, strip, 0)

    def far_turn(i):
        transform(low[i], low_t[i])
        if not two:
            transform(top[i], top_t[i])

    def third(i):
        weigh(low_t[i], 2, i)

    def fourth(i):
        weigh(low_t[i] if two else top_t[i], 3, i)

    def own_turn(i):
        own(i).wait_recv()
        transform(near[i].at[0], own_t[i] if two else near_t)

    def own_weigh(i):
        if not two:
            own_turn(i)
        weigh(own_t[i] if two else near_t, 1 - core, i)

    def sibling_far(i):
        passed(i, 2).wait_recv()
        transform(near[i].at[1], near_t)
        weigh(near_t, core, i)

    def arrived(step):
        for a in range(modes):
            share(step * modes + a).wait_recv()

    base = LAG * last + modes
    total = chunks + LAG * last
    plan = {
        base - 3: [(forward, 0)],
        base - 2: [(far_turn, 0)],
        base: [(arrived, 0)],
        base + 2: [(forward, 1), (far_turn, 1)],
        base + 3: [(arrived, 1), (own_weigh, 0), (own_weigh, 1), (sibling_far, 0)],
        base + 4: [(own_weigh, 2), (own_weigh, 3)],
        base + 5: [(sibling_far, 1)],
        base + 6: [(arrived, 2), (forward, 2), (third, 0)],
        base + 7: [(far_turn, 2), (third, 1)],
        base + 8: [(third, 2)],
        base + 9: [
            (forward, 3), (far_turn, 3), (third, 3), (sibling_far, 2), (sibling_far, 3),
            (arrived, 3), (fourth, 0), (fourth, 1), (fourth, 2), (fourth, 3),
        ],
    }
    if two:
        plan.update({1 + i: [(own_turn, i)] for i in range(pieces)})
    for copy in loads[2:]:
        copy.wait()
    for t in range(max(total, base + 10)):
        if t < total:
            tick(t)
        for task, which in plan.get(t, []):
            task(which)

    for i in range(pieces):
        far(i).wait_send()
        own(i).wait_send()
        passed(i, 2).wait_send()
        if not two:
            high(i).wait_send()

    def settle(q, carry):
        @pl.when(z < last)
        def _():
            rightward(q).wait_send()

        @pl.when(z > 0)
        def _():
            leftward(q).wait_send()

        share(q).wait_send()
        return carry

    lax.fori_loop(0, chunks, settle, 0)


def settled(total):
    rows = total.size // total.shape[-1]
    flat = total.reshape(rows, total.shape[-1])

    def move(src, dst, held, arrive, leave):
        size = held.shape[1]
        count = held.shape[0]
        bring = [pltpu.make_async_copy(src.at[pl.ds(i * size, size)], held.at[i], arrive.at[i]) for i in range(count)]
        take = [pltpu.make_async_copy(held.at[i], dst.at[pl.ds(i * size, size)], leave.at[i]) for i in range(count)]
        for i in range(count):
            bring[i].start()
        for i in range(count):
            bring[i].wait()
            take[i].start()
        for i in range(count):
            take[i].wait()

    parts = 8
    return pl.pallas_call(
        move,
        out_shape=jax.ShapeDtypeStruct(flat.shape, flat.dtype),
        in_specs=[pl.BlockSpec(memory_space=pl.ANY)],
        out_specs=pl.BlockSpec(memory_space=pl.ANY),
        scratch_shapes=[
            pltpu.VMEM((parts, rows // parts, flat.shape[1]), flat.dtype),
            pltpu.SemaphoreType.DMA((parts,)),
            pltpu.SemaphoreType.DMA((parts,)),
        ],
        compiler_params=pltpu.CompilerParams(vmem_limit_bytes=60 * 2**20),
        cost_estimate=pl.CostEstimate(flops=0, bytes_accessed=8 * 2**20, transcendentals=0),
    )(flat).reshape(total.shape)


def on_device(green_blocks, hopping, phonons, phonon_pick, momentum_offsets, energy_map):
    modes = hopping.shape[0]
    rows, cols = hopping.shape[1:]
    k_dev, e_dev, cells, parts = green_blocks.shape[:4]
    pieces = cells * parts
    chunks = STEPS * modes
    two = lax.axis_size("mom") == 4
    dma = pltpu.SemaphoreType.DMA
    vmem = pl.BlockSpec(memory_space=pltpu.VMEM)
    hbm = pl.BlockSpec(memory_space=pl.ANY)
    turned = pltpu.VMEM((modes, k_dev, e_dev, rows, cols), jnp.float32)
    total = pl.pallas_call(
        functools.partial(kernel, lax.axis_size("mom"), lax.axis_size("en")),
        out_shape=jax.ShapeDtypeStruct(green_blocks.shape, jnp.float32),
        in_specs=[hbm] * 6,
        out_specs=vmem,
        scratch_shapes=[
            pltpu.SMEM(phonon_pick.shape, jnp.int32),
            pltpu.SMEM(momentum_offsets.shape[::-1], jnp.int32),
            pltpu.SMEM(energy_map.shape[::-1], jnp.int32),
            pltpu.VMEM((modes * rows, cols), jnp.bfloat16),
            pltpu.VMEM((*phonons.shape[:3], rows // 2, cols), jnp.bfloat16),
            [pltpu.VMEM((2, k_dev, e_dev, rows, cols), jnp.bfloat16)] * pieces,
            [pltpu.VMEM((k_dev, e_dev, rows, cols), jnp.bfloat16)] * pieces,
            [pltpu.VMEM((k_dev, e_dev, rows, cols), jnp.bfloat16)] * (0 if two else pieces),
            [turned] * pieces,
            [turned] * (0 if two else pieces),
            [turned] * (pieces if two else 0),
            turned,
            pltpu.VMEM((chunks, 2, rows // 2, cols), jnp.bfloat16),
            pltpu.VMEM((chunks, 2, rows // 2, cols), jnp.bfloat16),
            pltpu.VMEM((chunks, 2, rows, cols), jnp.bfloat16),
            dma((5,)),
        ]
        + [dma((pieces,))] * 8
        + [dma((chunks,))] * 6,
        compiler_params=pltpu.CompilerParams(
            collective_id=0, has_side_effects=True, vmem_limit_bytes=(59 if two else 60) * 2**20
        ),
        cost_estimate=pl.CostEstimate(flops=13 * 10**9, bytes_accessed=8 * 2**20, transcendentals=0),
    )(
        phonon_pick, momentum_offsets.T, energy_map.T, green_blocks, hopping.reshape(-1, cols), phonons
    )
    return settled(total)


def solution(mesh):
    placed = (
        P(("groups", "mom"), "en", None, None, None, None),
        P("groups", None, None),
        P(("groups", "en"), None, None, None, None),
        P(),
        P(None, "mom"),
        P(None, "en"),
    )
    return jax.shard_map(
        on_device,
        mesh=mesh,
        in_specs=placed,
        out_specs=P(("groups", "mom"), "en", None, None, None, None),
        check_vma=False,
    )
```
